32 devices in a mesh: members: 2 (over y), tile: 4 (over z), group: 4 (over x, core).
Axes of the slice: x: 2, y: 2, z: 4, core: 2. Of those that a mesh axis runs over, the one named last changes fastest.
Arguments:
- theta: float32 [16, 16, 128], P('members', 'tile'), parts along dimension 0, may hold values from -6 to 6
- tracers: float32 [4, 96, 8, 16, 128], P('group', 'members', None, 'tile'), parts along dimension 1, may hold values from -6 to 6
- counts: int32 [4, 2], P('group', 'members'), parts along dimension 1, may hold values from 0 to 48, as said below
- flags: int32 [4, 96], P('group', 'members'), parts along dimension 1, may hold values 0 or 1
- kappa: float32 [4, 48], P('group'), may hold values from 0.02 to 0.2
Outputs:
- theta_out: float32 [16, 16, 128], P('members', 'tile'), parts along dimension 0
- tracers_out: float32 [4, 96, 8, 16, 128], P('group', 'members', None, 'tile'), parts along dimension 1
The draws below stay inside these ranges and needn't reach their ends.
There are 2 independent parts, one for each index of `members`. The reference program is written for one: setup_inputs(seed, part) draws one part's arguments, and reference() takes and returns one part's arrays. A program takes and returns all parts, laid end to end along the dimension named above; an argument that names none is the same for every part. Nothing has to cross between parts.
Inputs may be any that keep to these rules, and one draw needn't show every extreme that they name: counts[0, 0] is 0 (the dynamics group holds no tracers); every other group has 12 to 48 live slots, and some group has exactly 48.
All inputs are finite; a program needn't handle non-finite values. No bound on the sum of `flags` on one device may be relied on, other than what follows from the above.
Results may differ from the reference program's by a relative error of at most 0.00012.
Values sent between devices are 32-bit elements; how exact they have to be, the bound alone decides.
No kernel may reach another device: no remote copies, remote signals or barrier semaphores. Data moves between devices by JAX's collectives and lax.ppermute only.
A program may use at most 64 MiB of HBM per device.

```python
import math
import jax
import jax.numpy as jnp
from jax import lax

NY = 128
NZ = 8
TMAX = 48
STEPS = 3
INTERVALS = 2
GROUPS = 4
NX = 16


def draw_counts(key, part):
    first_key, second_key = jax.random.split(jax.random.fold_in(key, 17))
    values = jax.random.randint(first_key, (GROUPS,), 12, TMAX + 1)
    busiest = jax.random.randint(second_key, (), 1, GROUPS)
    places = jnp.arange(GROUPS)
    values = jnp.where(places == busiest, TMAX, values)
    values = jnp.where(places == 0, 0, values)
    return values.astype(jnp.int32).reshape(GROUPS, 1)


def with_ends(drawn, stream_key, low, largest):
    spot = [jax.random.randint(jax.random.fold_in(stream_key, axis), (), 0, length) for axis, length in enumerate(drawn.shape)]
    longest = drawn.shape.index(max(drawn.shape))
    beside = spot[:longest] + [(spot[longest] + 1) % drawn.shape[longest]] + spot[longest + 1:]
    return drawn.at[tuple(spot)].set(low).at[tuple(beside)].set(largest)


def block_levels(stream_key, shape, shards, low, high):
    def one(position, blocks):
        steps = jax.random.uniform(jax.random.fold_in(jax.random.fold_in(stream_key, 6), position), (blocks,), jnp.float32, low / len(shards), high / len(shards))
        return jnp.repeat(jnp.exp(steps), shape[position] // blocks).reshape((-1,) + (1,) * (len(shape) - position - 1))

    level = one(*shards[0])
    for cut in shards[1:]:
        level = level * one(*cut)
    return level


def gaussian(key, shape, width, bound, cuts=(), held_as=jnp.bfloat16):
    loudness = block_levels(key, shape, cuts, -0.22, 0.18) if cuts else 1.0
    result = jax.random.normal(key, shape, jnp.float32) * width * loudness
    return jnp.minimum(jnp.maximum(result, -bound), bound).astype(held_as)


def setup_inputs(seed: int = 0, part: int = 0) -> dict:
    key_of = jax.random.split(jax.random.key(seed), 6)
    part_splits = jax.random.split(jax.random.fold_in(key_of[5], part), 6)
    return {
        "theta": gaussian(part_splits[0], (NZ, NX, NY), 1.0, 6.0, ((1, 4),), jnp.float32),
        "tracers": gaussian(part_splits[1], (GROUPS, TMAX, NZ, NX, NY), 1.0, 6.0, ((0, 4), (3, 4)), jnp.float32),
        "counts": draw_counts(jax.random.fold_in(jax.random.fold_in(key_of[5], part), 71), part),
        "flags": with_ends((jax.random.randint(part_splits[3], (GROUPS, TMAX), 0, 2) < 1).astype(jnp.int32), jax.random.fold_in(part_splits[3], 1), 0, 1),
        "kappa": jnp.clip(jnp.exp(math.log(0.2) - 2.3025851 * jax.random.uniform(key_of[4], (GROUPS, TMAX), jnp.float32) ** block_levels(key_of[4], (GROUPS, TMAX), ((0, 4),), -0.2, 0.2)), 0.02, 0.2),
    }


wind_scale = 0.3
vert_scale = 0.2
mix_base = 0.08
heat_step = 0.3


def periodic_x(field):
    return jnp.concatenate([field[..., -1:, :], field, field[..., :1, :]], axis=-2)


def fields(theta_ext):
    center = theta_ext[:, 1:-1, :]
    grad_x = (theta_ext[:, 2:, :] - theta_ext[:, :-2, :]) * 0.5
    pad_y = jnp.pad(center, ((0, 0), (0, 0), (1, 1)))
    grad_y = (pad_y[:, :, 2:] - pad_y[:, :, :-2]) * 0.5
    pad_z = jnp.pad(center, ((1, 1), (0, 0), (0, 0)))
    grad_z = (pad_z[2:] - pad_z[:-2]) * 0.5
    wind_x = -wind_scale * grad_y
    wind_y = wind_scale * grad_x
    wind_z = vert_scale * grad_z
    mixing = mix_base * (1.0 + 0.5 * jnp.tanh(center))
    return wind_x, wind_y, wind_z, mixing


def tendency(extended, wind_x, wind_y, wind_z, mixing):
    center = extended[..., 1:-1, :]
    east = extended[..., 2:, :]
    west = extended[..., :-2, :]
    ndims = center.ndim
    pad_y = jnp.pad(center, [(0, 0)] * (ndims - 1) + [(1, 1)])
    north = pad_y[..., 2:]
    south = pad_y[..., :-2]
    pad_z = jnp.pad(center, [(0, 0)] * (ndims - 3) + [(1, 1), (0, 0), (0, 0)])
    upper = pad_z[..., 2:, :, :]
    lower = pad_z[..., :-2, :, :]
    advect = wind_x * (east - west) * 0.5 + wind_y * (north - south) * 0.5 + wind_z * (upper - lower) * 0.5
    return -advect + mixing * (east + west + north + south + upper + lower - 6.0 * center)


def reference(theta, tracers, counts, flags, kappa):
    slots = jnp.arange(TMAX, dtype=jnp.int32)
    live = (slots[None, :] < counts[:, 0:1]).astype(jnp.float32)
    weight = flags.astype(jnp.float32) * kappa * live
    state = tracers * live[:, :, None, None, None]
    for interval in range(INTERVALS):
        winds = fields(periodic_x(theta))
        for _ in range(STEPS):
            first = state + tendency(periodic_x(state), *winds)
            state = 0.5 * (state + first + tendency(periodic_x(first), *winds))
        heating = jnp.einsum("gt,gtzxy->zxy", weight, state, precision=lax.Precision.HIGHEST)
        theta = theta + heat_step * heating
    return theta, state
```

```python
import functools
import jax
import jax.numpy as jnp
from jax import lax
from jax.experimental import pallas as pl
from jax.experimental.pallas import tpu as pltpu
from jax.sharding import PartitionSpec as P

STEPS = 3
INTERVALS = 2

wind_scale = 0.3
vert_scale = 0.2
mix_base = 0.08
heat_step = 0.3

VMEM = pl.BlockSpec(memory_space=pltpu.VMEM)
SMEM = pl.BlockSpec(memory_space=pltpu.SMEM)
HBM = pl.BlockSpec(memory_space=pl.ANY)


def params():
    return pltpu.CompilerParams(vmem_limit_bytes=48 * 1024 * 1024)


def prepare(tiles, share, slots, me_ref, counts_ref, flags_ref, kappa_ref, theta_ref, tracers_ref, *outs):
    me = me_ref[0]
    count = counts_ref[0, 0]
    total = jnp.zeros(theta_ref.shape, jnp.float32)
    for step in range(tiles):
        block = lax.rem(me + step, tiles) * share
        for i in range(share):
            slot = block + i
            safe = jnp.minimum(slot, slots - 1)
            alive = slot < count
            field = tracers_ref[safe] * jnp.where(alive, 1.0, 0.0)
            weight = jnp.where(alive, flags_ref[0, safe].astype(jnp.float32) * kappa_ref[0, safe], 0.0)
            total = total + weight * field
            outs[step][i] = field
    for step in range(tiles):
        outs[step][share] = theta_ref[...]
        outs[step][share + 1] = total


def coefficients(theta_ref, coef_ref, length):
    shape = theta_ref.shape[1:]
    level = lax.broadcasted_iota(jnp.int32, shape, 0)
    place = lax.broadcasted_iota(jnp.int32, shape, 1)
    nz, ny = shape
    first_y, last_y = place > 0, place < ny - 1
    first_z, last_z = level > 0, level < nz - 1

    def body(x, carry):
        east = jnp.where(x == length - 1, 0, x + 1)
        west = jnp.where(x == 0, length - 1, x - 1)
        theta = theta_ref[x]
        grad_x = (theta_ref[east] - theta_ref[west]) * 0.5
        grad_y = (jnp.where(last_y, pltpu.roll(theta, ny - 1, 1), 0.0) - jnp.where(first_y, pltpu.roll(theta, 1, 1), 0.0)) * 0.5
        grad_z = (jnp.where(last_z, pltpu.roll(theta, nz - 1, 0), 0.0) - jnp.where(first_z, pltpu.roll(theta, 1, 0), 0.0)) * 0.5
        half_x = (-0.5 * wind_scale) * grad_y
        half_y = (0.5 * wind_scale) * grad_x
        half_z = (0.5 * vert_scale) * grad_z
        mixing = mix_base * (1.0 + 0.5 * jnp.tanh(theta))
        coef_ref[x, 0] = 1.0 - 6.0 * mixing
        coef_ref[x, 1] = mixing - half_x
        coef_ref[x, 2] = mixing + half_x
        coef_ref[x, 3] = jnp.where(last_y, mixing - half_y, 0.0)
        coef_ref[x, 4] = jnp.where(first_y, mixing + half_y, 0.0)
        coef_ref[x, 5] = jnp.where(last_z, mixing - half_z, 0.0)
        coef_ref[x, 6] = jnp.where(first_z, mixing + half_z, 0.0)
        return carry

    lax.fori_loop(0, length, body, 0, unroll=2)


def advance(coef_ref, state_ref, first_ref, length, count):
    nz, ny = state_ref.shape[-2:]

    def apply(source, x, east, west, i, coef):
        field = source[x, i]
        value = coef[0] * field + coef[1] * source[east, i] + coef[2] * source[west, i]
        value += coef[3] * pltpu.roll(field, ny - 1, 1) + coef[4] * pltpu.roll(field, 1, 1)
        value += coef[5] * pltpu.roll(field, nz - 1, 0) + coef[6] * pltpu.roll(field, 1, 0)
        return value

    def sweep(source, body_of):
        def body(x, carry):
            east = jnp.where(x == length - 1, 0, x + 1)
            west = jnp.where(x == 0, length - 1, x - 1)
            coef = [coef_ref[x, k] for k in range(7)]
            for i in range(count):
                body_of(x, i, apply(source, x, east, west, i, coef))
            return carry

        lax.fori_loop(0, length, body, 0, unroll=2)

    def put_first(x, i, value):
        first_ref[x, i] = value

    def put_state(x, i, value):
        state_ref[x, i] = state_ref[x, i] + value

    def step(_, carry):
        sweep(state_ref, put_first)
        sweep(first_ref, put_state)
        return carry

    lax.fori_loop(0, STEPS, step, 0)


def unpack(piece_ref, index, rows, nz, row):
    return piece_ref[index, pl.ds(row, nz, stride=rows), :]


def early(tiles, share, rows, nz, *refs):
    pieces, state_ref, coef_ref, theta_ref, first_ref = refs[:tiles], *refs[tiles:]
    length = tiles * rows
    for step in range(tiles):
        for row in range(rows):
            theta_ref[step * rows + row] = unpack(pieces[step], share, rows, nz, row)
            for i in range(share):
                state_ref[step * rows + row, i] = unpack(pieces[step], i, rows, nz, row)
    coefficients(theta_ref, coef_ref, length)
    advance(coef_ref, state_ref, first_ref, length, share)


def late(tiles, share, rows, nz, *refs):
    theta_in, total_in, held_ref = refs[:3]
    outs, theta_out = refs[3:3 + tiles], refs[3 + tiles]
    coef_ref, theta_ref, state_ref, first_ref, total_ref, next_ref = refs[4 + tiles:]
    length = tiles * rows
    scale = 0.5 ** STEPS
    for step in range(tiles):
        for row in range(rows):
            theta_ref[step * rows + row] = unpack(theta_in, step, rows, nz, row)
            total_ref[step * rows + row, 0] = unpack(total_in, step, rows, nz, row)
    coefficients(theta_ref, coef_ref, length)
    advance(coef_ref, total_ref, next_ref, length, 1)

    def heat(factor):
        def body(x, carry):
            theta_ref[x] = theta_ref[x] + (heat_step * factor) * total_ref[x, 0]
            return carry

        lax.fori_loop(0, length, body, 0, unroll=4)

    heat(scale)

    def copy(x, carry):
        for i in range(share):
            state_ref[x, i] = held_ref[x, i]
        state_ref[x, share] = total_ref[x, 0]
        return carry

    lax.fori_loop(0, length, copy, 0, unroll=2)
    coefficients(theta_ref, coef_ref, length)
    advance(coef_ref, state_ref, first_ref, length, share + 1)
    for step in range(tiles):
        for row in range(rows):
            x = step * rows + row
            for i in range(share):
                outs[step][i, pl.ds(row, nz, stride=rows), :] = state_ref[x, i] * (scale * scale)
            theta_out[step, pl.ds(row, nz, stride=rows), :] = theta_ref[x] + (heat_step * scale * scale) * state_ref[x, share]


def assemble(tiles, share, slots, me_ref, *refs):
    pieces, out_ref, sem = refs[:tiles], refs[tiles], refs[tiles + 1]
    me = me_ref[0]
    copies = []
    for step in range(tiles):
        block = lax.rem(me + tiles - step, tiles) * share
        copies.append(pltpu.make_async_copy(pieces[step], out_ref.at[pl.ds(block, share)], sem.at[step]))
        copies[-1].start()
    for copy in copies:
        copy.wait()


def butterfly(value, axis):
    size = lax.axis_size(axis)
    hop = 1
    while hop < size:
        value = value + lax.ppermute(value, axis, [(i, i ^ hop) for i in range(size)])
        hop *= 2
    return value


def per_device(theta, tracers, counts, flags, kappa):
    _, slots, nz, rows, ny = tracers.shape
    tiles = lax.axis_size("tile")
    share = -(-slots // tiles)
    length = tiles * rows
    me = lax.axis_index("tile").astype(jnp.int32).reshape(1)
    flat = (nz * rows, ny)
    f32 = jnp.float32
    field = lambda *lead: jax.ShapeDtypeStruct(lead, f32)

    def shift(value, step):
        return lax.ppermute(value, "tile", [(i, (i + step) % tiles) for i in range(tiles)])

    payload = pl.pallas_call(
        functools.partial(prepare, tiles, share, slots),
        out_shape=[field(share + 2, *flat)] * tiles,
        in_specs=[SMEM, SMEM, SMEM, SMEM, VMEM, VMEM],
        out_specs=[VMEM] * tiles,
        compiler_params=params(),
        name="prepare",
    )(me, counts, flags, kappa, theta.reshape(flat), tracers[0].reshape(slots, *flat))
    pieces = [payload[0]] + [shift(payload[tiles - step], tiles - step) for step in range(1, tiles)]
    total = butterfly(jnp.stack([piece[share + 1] for piece in pieces]), "group")
    grid_theta = jnp.stack([piece[share] for piece in pieces])

    held = pl.pallas_call(
        functools.partial(early, tiles, share, rows, nz),
        out_shape=field(length, share, nz, ny),
        in_specs=[VMEM] * tiles,
        out_specs=VMEM,
        scratch_shapes=[
            pltpu.VMEM((length, 7, nz, ny), f32),
            pltpu.VMEM((length, nz, ny), f32),
            pltpu.VMEM((length, share, nz, ny), f32),
        ],
        compiler_params=params(),
        name="early",
    )(*pieces)
    results = pl.pallas_call(
        functools.partial(late, tiles, share, rows, nz),
        out_shape=[field(share, *flat)] * tiles + [field(tiles, *flat)],
        in_specs=[VMEM] * 3,
        out_specs=[VMEM] * (tiles + 1),
        scratch_shapes=[
            pltpu.VMEM((length, 7, nz, ny), f32),
            pltpu.VMEM((length, nz, ny), f32),
            pltpu.VMEM((length, share + 1, nz, ny), f32),
            pltpu.VMEM((length, share + 1, nz, ny), f32),
            pltpu.VMEM((length, 1, nz, ny), f32),
            pltpu.VMEM((length, 1, nz, ny), f32),
        ],
        compiler_params=params(),
        name="late",
    )(grid_theta, total, held)
    back = [results[0]] + [shift(results[step], step) for step in range(1, tiles)]
    out = pl.pallas_call(
        functools.partial(assemble, tiles, share, slots),
        out_shape=field(tiles * share, *flat),
        in_specs=[SMEM] + [VMEM] * tiles,
        out_specs=HBM,
        scratch_shapes=[pltpu.SemaphoreType.DMA((tiles,))],
        compiler_params=params(),
        name="assemble",
    )(me, *back)
    theta_new = results[tiles][0].reshape(nz, rows, ny)
    return theta_new, out[:slots].reshape(1, slots, nz, rows, ny)


def solution(mesh):
    return jax.shard_map(
        per_device,
        mesh=mesh,
        in_specs=(
            P("members", "tile", None),
            P("group", "members", None, "tile", None),
            P("group", "members"),
            P("group", "members"),
            P("group", None),
        ),
        out_specs=(P("members", "tile", None), P("group", "members", None, "tile", None)),
        check_vma=False,
    )
```

```python
import functools
import jax
import jax.numpy as jnp
from jax import lax
from jax.experimental import pallas as pl
from jax.experimental.pallas import tpu as pltpu
from jax.sharding import PartitionSpec as P

STEPS = 3
INTERVALS = 2

wind_scale = 0.3
vert_scale = 0.2
mix_base = 0.08
heat_step = 0.3

UNROLL = 16
SCALE = 0.5 ** STEPS

VMEM = pl.BlockSpec(memory_space=pltpu.VMEM)
SMEM = pl.BlockSpec(memory_space=pltpu.SMEM)
HBM = pl.BlockSpec(memory_space=pltpu.HBM)


def params():
    return pltpu.CompilerParams(vmem_limit_bytes=48 * 1024 * 1024)


def cost(us):
    return pl.CostEstimate(flops=0, bytes_accessed=int(us * 1.0e3), transcendentals=0)


def prepare(tiles, parts, slots, me_ref, counts_ref, flags_hbm, kappa_hbm, theta_hbm, tracers_hbm, *refs):
    outs = refs[:tiles * len(parts)]
    flags_ref, kappa_ref, theta_ref, tracers_ref, sems = refs[tiles * len(parts):]
    copies = [
        pltpu.make_async_copy(source, target, sems.at[k])
        for k, (source, target) in enumerate(
            [(tracers_hbm, tracers_ref), (theta_hbm, theta_ref), (flags_hbm, flags_ref), (kappa_hbm, kappa_ref)]
        )
    ]
    for copy in copies:
        copy.start()
    for copy in copies:
        copy.wait()
    me = me_ref[0]
    count = counts_ref[0, 0]
    total = jnp.zeros(theta_ref.shape, jnp.float32)
    share = sum(parts)
    for step in range(tiles):
        block = lax.rem(me + step, tiles) * share
        before = 0
        for chunk, part in enumerate(parts):
            for i in range(part):
                slot = block + before + i
                safe = jnp.minimum(slot, slots - 1)
                alive = slot < count
                field = tracers_ref[safe] * jnp.where(alive, 1.0, 0.0)
                weight = jnp.where(alive, flags_ref[0, safe].astype(jnp.float32) * kappa_ref[0, safe], 0.0)
                total = total + weight * field
                outs[chunk * tiles + step][i] = field
            before += part
    for step in range(tiles):
        outs[step][parts[0]] = theta_ref[...]
        outs[step][parts[0] + 1] = total


def coefficients(theta_ref, coef_ref, length):
    shape = theta_ref.shape[1:]
    level = lax.broadcasted_iota(jnp.int32, shape, 0)
    place = lax.broadcasted_iota(jnp.int32, shape, 1)
    nz, ny = shape
    first_y, last_y = place > 0, place < ny - 1
    first_z, last_z = level > 0, level < nz - 1

    def body(x, carry):
        east = jnp.where(x == length - 1, 0, x + 1)
        west = jnp.where(x == 0, length - 1, x - 1)
        theta = theta_ref[x]
        grad_x = (theta_ref[east] - theta_ref[west]) * 0.5
        grad_y = (jnp.where(last_y, pltpu.roll(theta, ny - 1, 1), 0.0) - jnp.where(first_y, pltpu.roll(theta, 1, 1), 0.0)) * 0.5
        grad_z = (jnp.where(last_z, pltpu.roll(theta, nz - 1, 0), 0.0) - jnp.where(first_z, pltpu.roll(theta, 1, 0), 0.0)) * 0.5
        half_x = (-0.5 * wind_scale) * grad_y
        half_y = (0.5 * wind_scale) * grad_x
        half_z = (0.5 * vert_scale) * grad_z
        mixing = mix_base * (1.0 + 0.5 * jnp.tanh(theta))
        coef_ref[x, 0] = 1.0 - 6.0 * mixing
        coef_ref[x, 1] = mixing - half_x
        coef_ref[x, 2] = mixing + half_x
        coef_ref[x, 3] = jnp.where(last_y, mixing - half_y, 0.0)
        coef_ref[x, 4] = jnp.where(first_y, mixing + half_y, 0.0)
        coef_ref[x, 5] = jnp.where(last_z, mixing - half_z, 0.0)
        coef_ref[x, 6] = jnp.where(first_z, mixing + half_z, 0.0)
        return carry

    lax.fori_loop(0, length, body, 0, unroll=UNROLL)


def advance(coef_ref, state_ref, first_ref, length, count):
    nz, ny = state_ref.shape[-2:]

    def apply(source, x, east, west, i, coef):
        field = source[x, i]
        value = coef[0] * field + coef[1] * source[east, i] + coef[2] * source[west, i]
        value += coef[5] * pltpu.roll(field, nz - 1, 0) + coef[6] * pltpu.roll(field, 1, 0)
        value += coef[3] * pltpu.roll(field, ny - 1, 1) + coef[4] * pltpu.roll(field, 1, 1)
        return value

    def sweep(source, put):
        def body(x, carry):
            east = jnp.where(x == length - 1, 0, x + 1)
            west = jnp.where(x == 0, length - 1, x - 1)
            coef = [coef_ref[x, k] for k in range(7)]
            for i in range(count):
                put(x, i, apply(source, x, east, west, i, coef))
            return carry

        lax.fori_loop(0, length, body, 0, unroll=UNROLL)

    def put_first(x, i, value):
        first_ref[x, i] = value

    def put_state(x, i, value):
        state_ref[x, i] = state_ref[x, i] + value

    def step(_, carry):
        sweep(state_ref, put_first)
        sweep(first_ref, put_state)
        return carry

    lax.fori_loop(0, STEPS, step, 0)


def unpack(piece_ref, index, rows, nz, row):
    return piece_ref[index, pl.ds(row, nz, stride=rows), :]


def load(pieces, part, rows, nz, state_ref):
    for step, piece in enumerate(pieces):
        for row in range(rows):
            for i in range(part):
                state_ref[step * rows + row, i] = unpack(piece, i, rows, nz, row)


def store(outs, part, rows, nz, state_ref):
    for step, out in enumerate(outs):
        for row in range(rows):
            for i in range(part):
                out[i, pl.ds(row, nz, stride=rows), :] = state_ref[step * rows + row, i] * (SCALE * SCALE)


def early(tiles, part, rows, nz, *refs):
    pieces, (state_ref, coef_ref, theta_ref, first_ref) = refs[:tiles], refs[tiles:]
    for step in range(tiles):
        for row in range(rows):
            theta_ref[step * rows + row] = unpack(pieces[step], part, rows, nz, row)
    load(pieces, part, rows, nz, state_ref)
    coefficients(theta_ref, coef_ref, tiles * rows)
    advance(coef_ref, state_ref, first_ref, tiles * rows, part)


def dynamics(tiles, rows, nz, theta_in, total_in, coef_ref, coef_out, theta_out, state_ref, first_ref):
    length = tiles * rows
    for step in range(tiles):
        for row in range(rows):
            state_ref[step * rows + row, 0] = unpack(total_in, step, rows, nz, row)
    advance(coef_ref, state_ref, first_ref, length, 1)

    def heat(x, carry):
        theta_in[x] = theta_in[x] + (heat_step * SCALE) * state_ref[x, 0]
        return carry

    lax.fori_loop(0, length, heat, 0, unroll=UNROLL)
    coefficients(theta_in, coef_out, length)
    advance(coef_out, state_ref, first_ref, length, 1)
    for row in range(rows):
        theta_out[pl.ds(row, nz, stride=rows), :] = theta_in[row] + (heat_step * SCALE * SCALE) * state_ref[row, 0]


def dynamics_call(tiles, rows, nz, theta_pieces, total_in, coef_ref, coef_out, theta_out, state_ref, first_ref, theta_ref):
    for step in range(tiles):
        for row in range(rows):
            theta_ref[step * rows + row] = unpack(theta_pieces, step, rows, nz, row)
    dynamics(tiles, rows, nz, theta_ref, total_in, coef_ref, coef_out, theta_out, state_ref, first_ref)


def late(tiles, part, rows, nz, held_ref, coef_ref, *refs):
    outs, (state_ref, first_ref) = refs[:tiles], refs[tiles:]
    length = tiles * rows

    def copy(x, carry):
        for i in range(part):
            state_ref[x, i] = held_ref[x, i]
        return carry

    lax.fori_loop(0, length, copy, 0, unroll=UNROLL)
    advance(coef_ref, state_ref, first_ref, length, part)
    store(outs, part, rows, nz, state_ref)


def both(tiles, part, rows, nz, *refs):
    pieces, (coef_ref, next_ref) = refs[:tiles], refs[tiles:tiles + 2]
    outs, (state_ref, first_ref) = refs[tiles + 2:2 * tiles + 2], refs[2 * tiles + 2:]
    load(pieces, part, rows, nz, state_ref)
    advance(coef_ref, state_ref, first_ref, tiles * rows, part)
    advance(next_ref, state_ref, first_ref, tiles * rows, part)
    store(outs, part, rows, nz, state_ref)


def assemble(tiles, parts, me_ref, *refs):
    pieces, out_ref, sem = refs[:-2], refs[-2], refs[-1]
    me = me_ref[0]
    share = sum(parts)
    copies = []
    for step in range(tiles):
        slot = lax.rem(me + tiles - step, tiles) * share
        for chunk, part in enumerate(parts):
            copies.append(pltpu.make_async_copy(pieces[chunk * tiles + step], out_ref.at[pl.ds(slot, part)], sem.at[len(copies)]))
            copies[-1].start()
            slot = slot + part
    for copy in copies:
        copy.wait()


def butterfly(value, axis):
    size = lax.axis_size(axis)
    hop = 1
    while hop < size:
        value = value + lax.ppermute(value, axis, [(i, i ^ hop) for i in range(size)])
        hop *= 2
    return value


def per_device(theta, tracers, counts, flags, kappa):
    _, slots, nz, rows, ny = tracers.shape
    tiles = lax.axis_size("tile")
    share = max(2, -(-slots // tiles))
    parts = (share // 2, share - share // 2)
    length = tiles * rows
    me = lax.axis_index("tile").astype(jnp.int32).reshape(1)
    flat = (nz * rows, ny)
    f32 = jnp.float32
    field = lambda *lead: jax.ShapeDtypeStruct(lead, f32)
    scratch = lambda *lead: pltpu.VMEM(lead, f32)

    def shift(value, step):
        return lax.ppermute(value, "tile", [(i, (i + step) % tiles) for i in range(tiles)])

    def gather(payload):
        return [payload[0]] + [shift(payload[tiles - step], tiles - step) for step in range(1, tiles)]

    payload = pl.pallas_call(
        functools.partial(prepare, tiles, parts, slots),
        out_shape=[field(parts[0] + 2, *flat)] * tiles + [field(parts[1], *flat)] * tiles,
        in_specs=[SMEM, SMEM, HBM, HBM, HBM, HBM],
        out_specs=[VMEM] * (2 * tiles),
        scratch_shapes=[
            pltpu.SMEM(flags.shape, jnp.int32),
            pltpu.SMEM(kappa.shape, f32),
            scratch(*flat),
            scratch(slots, *flat),
            pltpu.SemaphoreType.DMA((4,)),
        ],
        compiler_params=params(),
        cost_estimate=cost(2),
        name="prepare",
    )(me, counts, flags, kappa, theta.reshape(flat), tracers[0].reshape(slots, *flat))
    one = gather(payload[:tiles])
    two = gather(payload[tiles:])
    total = butterfly(jnp.stack([piece[parts[0] + 1] for piece in one]), "group")
    grid_theta = jnp.stack([piece[parts[0]] for piece in one])

    held, coef = pl.pallas_call(
        functools.partial(early, tiles, parts[0], rows, nz),
        out_shape=[field(length, parts[0], nz, ny), field(length, 7, nz, ny)],
        in_specs=[VMEM] * tiles,
        out_specs=[VMEM] * 2,
        scratch_shapes=[scratch(length, nz, ny), scratch(length, parts[0], nz, ny)],
        compiler_params=params(),
        cost_estimate=cost(2.5),
        name="early",
    )(*one)
    next_coef, theta_new = pl.pallas_call(
        functools.partial(dynamics_call, tiles, rows, nz),
        out_shape=[field(length, 7, nz, ny), field(*flat)],
        in_specs=[VMEM] * 3,
        out_specs=[VMEM] * 2,
        scratch_shapes=[scratch(length, 1, nz, ny), scratch(length, 1, nz, ny), scratch(length, nz, ny)],
        compiler_params=params(),
        cost_estimate=cost(2.5),
        name="dynamics",
    )(grid_theta, total, coef)
    done_one = pl.pallas_call(
        functools.partial(late, tiles, parts[0], rows, nz),
        out_shape=[field(parts[0], *flat)] * tiles,
        in_specs=[VMEM] * 2,
        out_specs=[VMEM] * tiles,
        scratch_shapes=[scratch(length, parts[0], nz, ny)] * 2,
        compiler_params=params(),
        cost_estimate=cost(2),
        name="late",
    )(held, next_coef)
    done_two = pl.pallas_call(
        functools.partial(both, tiles, parts[1], rows, nz),
        out_shape=[field(parts[1], *flat)] * tiles,
        in_specs=[VMEM] * (tiles + 2),
        out_specs=[VMEM] * tiles,
        scratch_shapes=[scratch(length, parts[1], nz, ny)] * 2,
        compiler_params=params(),
        cost_estimate=cost(4),
        name="both",
    )(*two, coef, next_coef)
    back = [piece for done in (done_one, done_two) for piece in [done[0]] + [shift(done[step], step) for step in range(1, tiles)]]
    out = pl.pallas_call(
        functools.partial(assemble, tiles, parts),
        out_shape=field(tiles * share, *flat),
        in_specs=[SMEM] + [VMEM] * (2 * tiles),
        out_specs=HBM,
        scratch_shapes=[pltpu.SemaphoreType.DMA((2 * tiles,))],
        compiler_params=params(),
        cost_estimate=cost(1),
        name="assemble",
    )(me, *back)
    return theta_new.reshape(nz, rows, ny), out[:slots].reshape(1, slots, nz, rows, ny)


def solution(mesh):
    return jax.shard_map(
        per_device,
        mesh=mesh,
        in_specs=(
            P("members", "tile", None),
            P("group", "members", None, "tile", None),
            P("group", "members"),
            P("group", "members"),
            P("group", None),
        ),
        out_specs=(P("members", "tile", None), P("group", "members", None, "tile", None)),
        check_vma=False,
    )
```

```python
import functools
import jax
import jax.numpy as jnp
from jax import lax
from jax.experimental import pallas as pl
from jax.experimental.pallas import tpu as pltpu
from jax.sharding import PartitionSpec as P

STEPS = 3
INTERVALS = 2

wind_scale = 0.3
vert_scale = 0.2
mix_base = 0.08
heat_step = 0.3

UNROLL = 16
SCALE = 0.5 ** STEPS

VMEM = pl.BlockSpec(memory_space=pltpu.VMEM)
SMEM = pl.BlockSpec(memory_space=pltpu.SMEM)
HBM = pl.BlockSpec(memory_space=pl.ANY)


def params():
    return pltpu.CompilerParams(vmem_limit_bytes=48 * 1024 * 1024)


def weigh(slots, counts_ref, flags_ref, kappa_ref, tracers_ref, total_ref):
    count = counts_ref[0, 0]
    totals = [jnp.zeros(total_ref.shape, jnp.float32)] * 4
    for slot in range(slots):
        weight = jnp.where(slot < count, flags_ref[0, slot].astype(jnp.float32) * kappa_ref[0, slot], 0.0)
        totals[slot % 4] = totals[slot % 4] + weight * tracers_ref[slot]
    total_ref[...] = (totals[0] + totals[1]) + (totals[2] + totals[3])


def sort_slots(tiles, share, first, part, slots, me_ref, counts_ref, tracers_ref, outs):
    me = me_ref[0]
    count = counts_ref[0, 0]
    for step in range(tiles):
        block = lax.rem(me + step, tiles) * share + first
        for i in range(part):
            slot = block + i
            safe = jnp.minimum(slot, slots - 1)
            outs[step][i] = tracers_ref[safe] * jnp.where(slot < count, 1.0, 0.0)


def pack_one(tiles, share, part, slots, me_ref, counts_ref, tracers_ref, theta_ref, total_ref, other_ref, *outs):
    sort_slots(tiles, share, 0, part, slots, me_ref, counts_ref, tracers_ref, outs)
    for out in outs:
        out[part] = theta_ref[...]
        out[part + 1] = total_ref[...] + other_ref[...]


def pack_two(tiles, share, first, part, slots, me_ref, counts_ref, tracers_ref, after_ref, *outs):
    sort_slots(tiles, share, first, part, slots, me_ref, counts_ref, tracers_ref, outs)


def coefficients(theta_ref, coef_ref, length):
    shape = theta_ref.shape[1:]
    level = lax.broadcasted_iota(jnp.int32, shape, 0)
    place = lax.broadcasted_iota(jnp.int32, shape, 1)
    nz, ny = shape
    first_y, last_y = place > 0, place < ny - 1
    first_z, last_z = level > 0, level < nz - 1

    def body(x, carry):
        east = jnp.where(x == length - 1, 0, x + 1)
        west = jnp.where(x == 0, length - 1, x - 1)
        theta = theta_ref[x]
        grad_x = (theta_ref[east] - theta_ref[west]) * 0.5
        grad_y = (jnp.where(last_y, pltpu.roll(theta, ny - 1, 1), 0.0) - jnp.where(first_y, pltpu.roll(theta, 1, 1), 0.0)) * 0.5
        grad_z = (jnp.where(last_z, pltpu.roll(theta, nz - 1, 0), 0.0) - jnp.where(first_z, pltpu.roll(theta, 1, 0), 0.0)) * 0.5
        half_x = (-0.5 * wind_scale) * grad_y
        half_y = (0.5 * wind_scale) * grad_x
        half_z = (0.5 * vert_scale) * grad_z
        mixing = mix_base * (1.0 + 0.5 * jnp.tanh(theta))
        coef_ref[x, 0] = 1.0 - 6.0 * mixing
        coef_ref[x, 1] = mixing - half_x
        coef_ref[x, 2] = mixing + half_x
        coef_ref[x, 3] = jnp.where(last_y, mixing - half_y, 0.0)
        coef_ref[x, 4] = jnp.where(first_y, mixing + half_y, 0.0)
        coef_ref[x, 5] = jnp.where(last_z, mixing - half_z, 0.0)
        coef_ref[x, 6] = jnp.where(first_z, mixing + half_z, 0.0)
        return carry

    lax.fori_loop(0, length, body, 0, unroll=UNROLL)


def advance(coef_ref, state_ref, first_ref, length, count):
    nz, ny = state_ref.shape[-2:]

    def apply(source, x, east, west, i, coef):
        field = source[x, i]
        value = coef[0] * field + coef[1] * source[east, i] + coef[2] * source[west, i]
        value += coef[5] * pltpu.roll(field, nz - 1, 0) + coef[6] * pltpu.roll(field, 1, 0)
        value += coef[3] * pltpu.roll(field, ny - 1, 1) + coef[4] * pltpu.roll(field, 1, 1)
        return value

    def sweep(source, put):
        def body(x, carry):
            east = jnp.where(x == length - 1, 0, x + 1)
            west = jnp.where(x == 0, length - 1, x - 1)
            coef = [coef_ref[x, k] for k in range(7)]
            for i in range(count):
                put(x, i, apply(source, x, east, west, i, coef))
            return carry

        lax.fori_loop(0, length, body, 0, unroll=UNROLL)

    def put_first(x, i, value):
        first_ref[x, i] = value

    def put_state(x, i, value):
        state_ref[x, i] = state_ref[x, i] + value

    def step(_, carry):
        sweep(state_ref, put_first)
        sweep(first_ref, put_state)
        return carry

    lax.fori_loop(0, STEPS, step, 0)


def unpack(piece_ref, index, rows, nz, row):
    return piece_ref[index, pl.ds(row, nz, stride=rows), :]


def load(pieces, part, rows, nz, state_ref):
    for step, piece in enumerate(pieces):
        for row in range(rows):
            for i in range(part):
                state_ref[step * rows + row, i] = unpack(piece, i, rows, nz, row)


def store(outs, part, rows, nz, state_ref):
    for step, out in enumerate(outs):
        for row in range(rows):
            for i in range(part):
                out[i, pl.ds(row, nz, stride=rows), :] = state_ref[step * rows + row, i] * (SCALE * SCALE)


def early(tiles, part, rows, nz, *refs):
    pieces, (state_ref, coef_ref, theta_ref, first_ref) = refs[:tiles], refs[tiles:]
    for step in range(tiles):
        for row in range(rows):
            theta_ref[step * rows + row] = unpack(pieces[step], part, rows, nz, row)
    load(pieces, part, rows, nz, state_ref)
    coefficients(theta_ref, coef_ref, tiles * rows)
    advance(coef_ref, state_ref, first_ref, tiles * rows, part)


def dynamics(tiles, rows, nz, theta_in, total_in, coef_ref, coef_out, theta_out, state_ref, first_ref):
    length = tiles * rows
    for step in range(tiles):
        for row in range(rows):
            state_ref[step * rows + row, 0] = unpack(total_in, step, rows, nz, row)
    advance(coef_ref, state_ref, first_ref, length, 1)

    def heat(x, carry):
        theta_in[x] = theta_in[x] + (heat_step * SCALE) * state_ref[x, 0]
        return carry

    lax.fori_loop(0, length, heat, 0, unroll=UNROLL)
    coefficients(theta_in, coef_out, length)
    advance(coef_out, state_ref, first_ref, length, 1)
    for row in range(rows):
        theta_out[pl.ds(row, nz, stride=rows), :] = theta_in[row] + (heat_step * SCALE * SCALE) * state_ref[row, 0]


def dynamics_call(tiles, rows, nz, theta_pieces, total_in, coef_ref, coef_out, theta_out, state_ref, first_ref, theta_ref):
    for step in range(tiles):
        for row in range(rows):
            theta_ref[step * rows + row] = unpack(theta_pieces, step, rows, nz, row)
    dynamics(tiles, rows, nz, theta_ref, total_in, coef_ref, coef_out, theta_out, state_ref, first_ref)


def late(tiles, part, rows, nz, held_ref, coef_ref, *refs):
    outs, (state_ref, first_ref) = refs[:tiles], refs[tiles:]
    length = tiles * rows

    def copy(x, carry):
        for i in range(part):
            state_ref[x, i] = held_ref[x, i]
        return carry

    lax.fori_loop(0, length, copy, 0, unroll=UNROLL)
    advance(coef_ref, state_ref, first_ref, length, part)
    store(outs, part, rows, nz, state_ref)


def both(tiles, part, rows, nz, *refs):
    pieces, (coef_ref, next_ref) = refs[:tiles], refs[tiles:tiles + 2]
    outs, (state_ref, first_ref) = refs[tiles + 2:2 * tiles + 2], refs[2 * tiles + 2:]
    load(pieces, part, rows, nz, state_ref)
    advance(coef_ref, state_ref, first_ref, tiles * rows, part)
    advance(next_ref, state_ref, first_ref, tiles * rows, part)
    store(outs, part, rows, nz, state_ref)


def assemble(tiles, parts, me_ref, *refs):
    pieces, out_ref, sem = refs[:-2], refs[-2], refs[-1]
    me = me_ref[0]
    share = sum(parts)
    copies = []
    for step in range(tiles):
        slot = lax.rem(me + tiles - step, tiles) * share
        for chunk, part in enumerate(parts):
            copies.append(pltpu.make_async_copy(pieces[chunk * tiles + step], out_ref.at[pl.ds(slot, part)], sem.at[len(copies)]))
            copies[-1].start()
            slot = slot + part
    for copy in copies:
        copy.wait()


def swap(value, axis, hop):
    return lax.ppermute(value, axis, [(i, i ^ hop) for i in range(lax.axis_size(axis))])


def per_device(theta, tracers, counts, flags, kappa):
    _, slots, nz, rows, ny = tracers.shape
    tiles = lax.axis_size("tile")
    share = max(2, -(-slots // tiles))
    parts = (share // 2, share - share // 2)
    length = tiles * rows
    me = lax.axis_index("tile").astype(jnp.int32).reshape(1)
    flat = (nz * rows, ny)
    f32 = jnp.float32
    field = lambda *lead: jax.ShapeDtypeStruct(lead, f32)
    scratch = lambda *lead: pltpu.VMEM(lead, f32)

    def shift(value, step):
        return lax.ppermute(value, "tile", [(i, (i + step) % tiles) for i in range(tiles)])

    def gather(payload):
        return [payload[0]] + [shift(payload[tiles - step], tiles - step) for step in range(1, tiles)]

    tracers = tracers[0].reshape(slots, *flat)
    theta = theta.reshape(flat)
    total = pl.pallas_call(
        functools.partial(weigh, slots),
        out_shape=field(*flat),
        in_specs=[SMEM, SMEM, SMEM, VMEM],
        out_specs=VMEM,
        compiler_params=params(),
        name="weigh",
    )(counts, flags, kappa, tracers)
    one = gather(pl.pallas_call(
        functools.partial(pack_one, tiles, share, parts[0], slots),
        out_shape=[field(parts[0] + 2, *flat)] * tiles,
        in_specs=[SMEM, SMEM] + [VMEM] * 4,
        out_specs=[VMEM] * tiles,
        compiler_params=params(),
        name="pack_one",
    )(me, counts, tracers, theta, total, swap(total, "group", 1)))
    two = gather(pl.pallas_call(
        functools.partial(pack_two, tiles, share, parts[0], parts[1], slots),
        out_shape=[field(parts[1], *flat)] * tiles,
        in_specs=[SMEM, SMEM, VMEM, HBM],
        out_specs=[VMEM] * tiles,
        compiler_params=params(),
        name="pack_two",
    )(me, counts, tracers, one[0]))
    total = jnp.stack([piece[parts[0] + 1] for piece in one])
    hop = 2
    while hop < lax.axis_size("group"):
        total = total + swap(total, "group", hop)
        hop *= 2
    grid_theta = jnp.stack([piece[parts[0]] for piece in one])

    held, coef = pl.pallas_call(
        functools.partial(early, tiles, parts[0], rows, nz),
        out_shape=[field(length, parts[0], nz, ny), field(length, 7, nz, ny)],
        in_specs=[VMEM] * tiles,
        out_specs=[VMEM] * 2,
        scratch_shapes=[scratch(length, nz, ny), scratch(length, parts[0], nz, ny)],
        compiler_params=params(),
        name="early",
    )(*one)
    next_coef, theta_new = pl.pallas_call(
        functools.partial(dynamics_call, tiles, rows, nz),
        out_shape=[field(length, 7, nz, ny), field(*flat)],
        in_specs=[VMEM] * 3,
        out_specs=[VMEM] * 2,
        scratch_shapes=[scratch(length, 1, nz, ny), scratch(length, 1, nz, ny), scratch(length, nz, ny)],
        compiler_params=params(),
        name="dynamics",
    )(grid_theta, total, coef)
    done_one = pl.pallas_call(
        functools.partial(late, tiles, parts[0], rows, nz),
        out_shape=[field(parts[0], *flat)] * tiles,
        in_specs=[VMEM] * 2,
        out_specs=[VMEM] * tiles,
        scratch_shapes=[scratch(length, parts[0], nz, ny)] * 2,
        compiler_params=params(),
        name="late",
    )(held, next_coef)
    done_two = pl.pallas_call(
        functools.partial(both, tiles, parts[1], rows, nz),
        out_shape=[field(parts[1], *flat)] * tiles,
        in_specs=[VMEM] * (tiles + 2),
        out_specs=[VMEM] * tiles,
        scratch_shapes=[scratch(length, parts[1], nz, ny)] * 2,
        compiler_params=params(),
        name="both",
    )(*two, coef, next_coef)
    back = [piece for done in (done_one, done_two) for piece in [done[0]] + [shift(done[step], step) for step in range(1, tiles)]]
    out = pl.pallas_call(
        functools.partial(assemble, tiles, parts),
        out_shape=field(tiles * share, *flat),
        in_specs=[SMEM] + [VMEM] * (2 * tiles),
        out_specs=HBM,
        scratch_shapes=[pltpu.SemaphoreType.DMA((2 * tiles,))],
        compiler_params=params(),
        name="assemble",
    )(me, *back)
    return theta_new.reshape(nz, rows, ny), out[:slots].reshape(1, slots, nz, rows, ny)


def solution(mesh):
    return jax.shard_map(
        per_device,
        mesh=mesh,
        in_specs=(
            P("members", "tile", None),
            P("group", "members", None, "tile", None),
            P("group", "members"),
            P("group", "members"),
            P("group", None),
        ),
        out_specs=(P("members", "tile", None), P("group", "members", None, "tile", None)),
        check_vma=False,
    )
```

```python
import functools
import jax
import jax.numpy as jnp
from jax import lax
from jax.experimental import pallas as pl
from jax.experimental.pallas import tpu as pltpu
from jax.sharding import PartitionSpec as P

STEPS = 3
INTERVALS = 2

wind_scale = 0.3
vert_scale = 0.2
mix_base = 0.08
heat_step = 0.3

UNROLL = 16
SCALE = 0.5 ** STEPS

VMEM = pl.BlockSpec(memory_space=pltpu.VMEM)
SMEM = pl.BlockSpec(memory_space=pltpu.SMEM)
HBM = pl.BlockSpec(memory_space=pl.ANY)


def params():
    return pltpu.CompilerParams(vmem_limit_bytes=48 * 1024 * 1024)


def weigh(slots, counts_ref, flags_ref, kappa_ref, tracers_ref, total_ref):
    count = counts_ref[0, 0]
    totals = [jnp.zeros(total_ref.shape, jnp.float32)] * 4
    for slot in range(slots):
        weight = jnp.where(slot < count, flags_ref[0, slot].astype(jnp.float32) * kappa_ref[0, slot], 0.0)
        totals[slot % 4] = totals[slot % 4] + weight * tracers_ref[slot]
    total_ref[...] = (totals[0] + totals[1]) + (totals[2] + totals[3])


def sort_slots(tiles, share, first, part, slots, me_ref, counts_ref, tracers_ref, outs):
    me = me_ref[0]
    count = counts_ref[0, 0]
    for step in range(tiles):
        block = lax.rem(me + step, tiles) * share + first
        for i in range(part):
            slot = block + i
            safe = jnp.minimum(slot, slots - 1)
            outs[step][i] = tracers_ref[safe] * jnp.where(slot < count, 1.0, 0.0)


def pack_one(tiles, share, part, slots, me_ref, counts_ref, tracers_ref, theta_ref, total_ref, other_ref, *outs):
    sort_slots(tiles, share, 0, part, slots, me_ref, counts_ref, tracers_ref, outs)
    for out in outs:
        out[part] = theta_ref[...]
        out[part + 1] = total_ref[...] + other_ref[...]


def pack_two(tiles, share, first, part, slots, me_ref, counts_ref, tracers_ref, after_ref, *outs):
    sort_slots(tiles, share, first, part, slots, me_ref, counts_ref, tracers_ref, outs)


def coefficients(theta_ref, coef_ref, length):
    shape = theta_ref.shape[1:]
    level = lax.broadcasted_iota(jnp.int32, shape, 0)
    place = lax.broadcasted_iota(jnp.int32, shape, 1)
    nz, ny = shape
    first_y, last_y = place > 0, place < ny - 1
    first_z, last_z = level > 0, level < nz - 1

    def body(x, carry):
        east = jnp.where(x == length - 1, 0, x + 1)
        west = jnp.where(x == 0, length - 1, x - 1)
        theta = theta_ref[x]
        grad_x = (theta_ref[east] - theta_ref[west]) * 0.5
        grad_y = (jnp.where(last_y, pltpu.roll(theta, ny - 1, 1), 0.0) - jnp.where(first_y, pltpu.roll(theta, 1, 1), 0.0)) * 0.5
        grad_z = (jnp.where(last_z, pltpu.roll(theta, nz - 1, 0), 0.0) - jnp.where(first_z, pltpu.roll(theta, 1, 0), 0.0)) * 0.5
        half_x = (-0.5 * wind_scale) * grad_y
        half_y = (0.5 * wind_scale) * grad_x
        half_z = (0.5 * vert_scale) * grad_z
        mixing = mix_base * (1.0 + 0.5 * jnp.tanh(theta))
        coef_ref[x, 0] = 1.0 - 6.0 * mixing
        coef_ref[x, 1] = mixing - half_x
        coef_ref[x, 2] = mixing + half_x
        coef_ref[x, 3] = jnp.where(last_y, mixing - half_y, 0.0)
        coef_ref[x, 4] = jnp.where(first_y, mixing + half_y, 0.0)
        coef_ref[x, 5] = jnp.where(last_z, mixing - half_z, 0.0)
        coef_ref[x, 6] = jnp.where(first_z, mixing + half_z, 0.0)
        return carry

    lax.fori_loop(0, length, body, 0, unroll=UNROLL)


def advance(coef_ref, state_ref, first_ref, length, count):
    nz, ny = state_ref.shape[-2:]

    def apply(source, x, east, west, i, coef):
        field = source[x, i]
        value = coef[0] * field + coef[1] * source[east, i] + coef[2] * source[west, i]
        value += coef[5] * pltpu.roll(field, nz - 1, 0) + coef[6] * pltpu.roll(field, 1, 0)
        value += coef[3] * pltpu.roll(field, ny - 1, 1) + coef[4] * pltpu.roll(field, 1, 1)
        return value

    def sweep(source, put):
        def body(x, carry):
            east = jnp.where(x == length - 1, 0, x + 1)
            west = jnp.where(x == 0, length - 1, x - 1)
            coef = [coef_ref[x, k] for k in range(7)]
            for i in range(count):
                put(x, i, apply(source, x, east, west, i, coef))
            return carry

        lax.fori_loop(0, length, body, 0, unroll=UNROLL)

    def put_first(x, i, value):
        first_ref[x, i] = value

    def put_state(x, i, value):
        state_ref[x, i] = state_ref[x, i] + value

    def step(_, carry):
        sweep(state_ref, put_first)
        sweep(first_ref, put_state)
        return carry

    lax.fori_loop(0, STEPS, step, 0)


def unpack(piece_ref, index, rows, nz, row):
    return piece_ref[index, pl.ds(row, nz, stride=rows), :]


def load(pieces, part, rows, nz, state_ref):
    for step, piece in enumerate(pieces):
        for row in range(rows):
            for i in range(part):
                state_ref[step * rows + row, i] = unpack(piece, i, rows, nz, row)


def store(outs, part, rows, nz, state_ref):
    for step, out in enumerate(outs):
        for row in range(rows):
            for i in range(part):
                out[i, pl.ds(row, nz, stride=rows), :] = state_ref[step * rows + row, i] * (SCALE * SCALE)


def early(tiles, part, rows, nz, *refs):
    pieces, (state_ref, coef_ref, theta_ref, first_ref) = refs[:tiles], refs[tiles:]
    for step in range(tiles):
        for row in range(rows):
            theta_ref[step * rows + row] = unpack(pieces[step], part, rows, nz, row)
    load(pieces, part, rows, nz, state_ref)
    coefficients(theta_ref, coef_ref, tiles * rows)
    advance(coef_ref, state_ref, first_ref, tiles * rows, part)


def dynamics(tiles, rows, nz, theta_in, total_in, coef_ref, coef_out, theta_out, state_ref, first_ref):
    length = tiles * rows
    for step in range(tiles):
        for row in range(rows):
            state_ref[step * rows + row, 0] = unpack(total_in, step, rows, nz, row)
    advance(coef_ref, state_ref, first_ref, length, 1)

    def heat(x, carry):
        theta_in[x] = theta_in[x] + (heat_step * SCALE) * state_ref[x, 0]
        return carry

    lax.fori_loop(0, length, heat, 0, unroll=UNROLL)
    coefficients(theta_in, coef_out, length)
    advance(coef_out, state_ref, first_ref, length, 1)
    for row in range(rows):
        theta_out[pl.ds(row, nz, stride=rows), :] = theta_in[row] + (heat_step * SCALE * SCALE) * state_ref[row, 0]


def dynamics_call(tiles, rows, nz, theta_pieces, total_in, coef_ref, coef_out, theta_out, state_ref, first_ref, theta_ref):
    for step in range(tiles):
        for row in range(rows):
            theta_ref[step * rows + row] = unpack(theta_pieces, step, rows, nz, row)
    dynamics(tiles, rows, nz, theta_ref, total_in, coef_ref, coef_out, theta_out, state_ref, first_ref)


def late(tiles, part, rows, nz, held_ref, coef_ref, *refs):
    outs, (state_ref, first_ref) = refs[:tiles], refs[tiles:]
    length = tiles * rows

    def copy(x, carry):
        for i in range(part):
            state_ref[x, i] = held_ref[x, i]
        return carry

    lax.fori_loop(0, length, copy, 0, unroll=UNROLL)
    advance(coef_ref, state_ref, first_ref, length, part)
    store(outs, part, rows, nz, state_ref)


def both(tiles, part, rows, nz, *refs):
    pieces, (coef_ref, next_ref) = refs[:tiles], refs[tiles:tiles + 2]
    outs, (state_ref, first_ref) = refs[tiles + 2:2 * tiles + 2], refs[2 * tiles + 2:]
    load(pieces, part, rows, nz, state_ref)
    advance(coef_ref, state_ref, first_ref, tiles * rows, part)
    advance(next_ref, state_ref, first_ref, tiles * rows, part)
    store(outs, part, rows, nz, state_ref)


def assemble(tiles, parts, me_ref, *refs):
    pieces, out_ref, sem = refs[:-2], refs[-2], refs[-1]
    me = me_ref[0]
    share = sum(parts)
    copies = []
    for step in range(tiles):
        slot = lax.rem(me + tiles - step, tiles) * share
        for chunk, part in enumerate(parts):
            copies.append(pltpu.make_async_copy(pieces[chunk * tiles + step], out_ref.at[pl.ds(slot, part)], sem.at[len(copies)]))
            copies[-1].start()
            slot = slot + part
    for copy in copies:
        copy.wait()


def swap(value, axis, hop):
    return lax.ppermute(value, axis, [(i, i ^ hop) for i in range(lax.axis_size(axis))])


def per_device(theta, tracers, counts, flags, kappa):
    _, slots, nz, rows, ny = tracers.shape
    tiles = lax.axis_size("tile")
    share = max(2, -(-slots // tiles))
    parts = (max(1, share // 3), share - max(1, share // 3))
    length = tiles * rows
    me = lax.axis_index("tile").astype(jnp.int32).reshape(1)
    flat = (nz * rows, ny)
    f32 = jnp.float32
    field = lambda *lead: jax.ShapeDtypeStruct(lead, f32)
    scratch = lambda *lead: pltpu.VMEM(lead, f32)

    def shift(value, step):
        return lax.ppermute(value, "tile", [(i, (i + step) % tiles) for i in range(tiles)])

    def gather(payload):
        return [payload[0]] + [shift(payload[tiles - step], tiles - step) for step in range(1, tiles)]

    tracers = tracers[0].reshape(slots, *flat)
    theta = theta.reshape(flat)
    total = pl.pallas_call(
        functools.partial(weigh, slots),
        out_shape=field(*flat),
        in_specs=[SMEM, SMEM, SMEM, VMEM],
        out_specs=VMEM,
        compiler_params=params(),
        name="weigh",
    )(counts, flags, kappa, tracers)
    one = gather(pl.pallas_call(
        functools.partial(pack_one, tiles, share, parts[0], slots),
        out_shape=[field(parts[0] + 2, *flat)] * tiles,
        in_specs=[SMEM, SMEM] + [VMEM] * 4,
        out_specs=[VMEM] * tiles,
        compiler_params=params(),
        name="pack_one",
    )(me, counts, tracers, theta, total, swap(total, "group", 1)))
    two = gather(pl.pallas_call(
        functools.partial(pack_two, tiles, share, parts[0], parts[1], slots),
        out_shape=[field(parts[1], *flat)] * tiles,
        in_specs=[SMEM, SMEM, VMEM, HBM],
        out_specs=[VMEM] * tiles,
        compiler_params=params(),
        name="pack_two",
    )(me, counts, tracers, one[0]))
    total = jnp.stack([piece[parts[0] + 1] for piece in one])
    hop = 2
    while hop < lax.axis_size("group"):
        total = total + swap(total, "group", hop)
        hop *= 2
    grid_theta = jnp.stack([piece[parts[0]] for piece in one])

    held, coef = pl.pallas_call(
        functools.partial(early, tiles, parts[0], rows, nz),
        out_shape=[field(length, parts[0], nz, ny), field(length, 7, nz, ny)],
        in_specs=[VMEM] * tiles,
        out_specs=[VMEM] * 2,
        scratch_shapes=[scratch(length, nz, ny), scratch(length, parts[0], nz, ny)],
        compiler_params=params(),
        name="early",
    )(*one)
    next_coef, theta_new = pl.pallas_call(
        functools.partial(dynamics_call, tiles, rows, nz),
        out_shape=[field(length, 7, nz, ny), field(*flat)],
        in_specs=[VMEM] * 3,
        out_specs=[VMEM] * 2,
        scratch_shapes=[scratch(length, 1, nz, ny), scratch(length, 1, nz, ny), scratch(length, nz, ny)],
        compiler_params=params(),
        name="dynamics",
    )(grid_theta, total, coef)
    done_one = pl.pallas_call(
        functools.partial(late, tiles, parts[0], rows, nz),
        out_shape=[field(parts[0], *flat)] * tiles,
        in_specs=[VMEM] * 2,
        out_specs=[VMEM] * tiles,
        scratch_shapes=[scratch(length, parts[0], nz, ny)] * 2,
        compiler_params=params(),
        name="late",
    )(held, next_coef)
    done_two = pl.pallas_call(
        functools.partial(both, tiles, parts[1], rows, nz),
        out_shape=[field(parts[1], *flat)] * tiles,
        in_specs=[VMEM] * (tiles + 2),
        out_specs=[VMEM] * tiles,
        scratch_shapes=[scratch(length, parts[1], nz, ny)] * 2,
        compiler_params=params(),
        name="both",
    )(*two, coef, next_coef)
    back = [piece for done in (done_one, done_two) for piece in [done[0]] + [shift(done[step], step) for step in range(1, tiles)]]
    out = pl.pallas_call(
        functools.partial(assemble, tiles, parts),
        out_shape=field(tiles * share, *flat),
        in_specs=[SMEM] + [VMEM] * (2 * tiles),
        out_specs=HBM,
        scratch_shapes=[pltpu.SemaphoreType.DMA((2 * tiles,))],
        compiler_params=params(),
        name="assemble",
    )(me, *back)
    return theta_new.reshape(nz, rows, ny), out[:slots].reshape(1, slots, nz, rows, ny)


def solution(mesh):
    return jax.shard_map(
        per_device,
        mesh=mesh,
        in_specs=(
            P("members", "tile", None),
            P("group", "members", None, "tile", None),
            P("group", "members"),
            P("group", "members"),
            P("group", None),
        ),
        out_specs=(P("members", "tile", None), P("group", "members", None, "tile", None)),
        check_vma=False,
    )
```

```python
import functools
import jax
import jax.numpy as jnp
from jax import lax
from jax.experimental import pallas as pl
from jax.experimental.pallas import tpu as pltpu
from jax.sharding import PartitionSpec as P

STEPS = 3
INTERVALS = 2

wind_scale = 0.3
vert_scale = 0.2
mix_base = 0.08
heat_step = 0.3

UNROLL = 16
SCALE = 0.5 ** STEPS

VMEM = pl.BlockSpec(memory_space=pltpu.VMEM)
SMEM = pl.BlockSpec(memory_space=pltpu.SMEM)
HBM = pl.BlockSpec(memory_space=pl.ANY)


def params():
    return pltpu.CompilerParams(vmem_limit_bytes=48 * 1024 * 1024)


def weigh(slots, counts_ref, flags_ref, kappa_ref, tracers_ref, total_ref):
    count = counts_ref[0, 0]
    totals = [jnp.zeros(total_ref.shape, jnp.float32)] * 4
    for slot in range(slots):
        weight = jnp.where(slot < count, flags_ref[0, slot].astype(jnp.float32) * kappa_ref[0, slot], 0.0)
        totals[slot % 4] = totals[slot % 4] + weight * tracers_ref[slot]
    total_ref[...] = (totals[0] + totals[1]) + (totals[2] + totals[3])


def sort_slots(tiles, share, first, part, slots, me_ref, counts_ref, tracers_ref, outs):
    me = me_ref[0]
    count = counts_ref[0, 0]
    for step in range(tiles):
        block = lax.rem(me + step, tiles) * share + first
        for i in range(part):
            slot = block + i
            safe = jnp.minimum(slot, slots - 1)
            outs[step][i] = tracers_ref[safe] * jnp.where(slot < count, 1.0, 0.0)


def pack_two(tiles, share, first, part, slots, me_ref, counts_ref, tracers_ref, after_ref, *outs):
    sort_slots(tiles, share, first, part, slots, me_ref, counts_ref, tracers_ref, outs)


def coefficients(theta_ref, coef_ref, length):
    shape = theta_ref.shape[1:]
    level = lax.broadcasted_iota(jnp.int32, shape, 0)
    place = lax.broadcasted_iota(jnp.int32, shape, 1)
    nz, ny = shape
    first_y, last_y = place > 0, place < ny - 1
    first_z, last_z = level > 0, level < nz - 1

    def body(x, carry):
        east = jnp.where(x == length - 1, 0, x + 1)
        west = jnp.where(x == 0, length - 1, x - 1)
        theta = theta_ref[x]
        grad_x = (theta_ref[east] - theta_ref[west]) * 0.5
        grad_y = (jnp.where(last_y, pltpu.roll(theta, ny - 1, 1), 0.0) - jnp.where(first_y, pltpu.roll(theta, 1, 1), 0.0)) * 0.5
        grad_z = (jnp.where(last_z, pltpu.roll(theta, nz - 1, 0), 0.0) - jnp.where(first_z, pltpu.roll(theta, 1, 0), 0.0)) * 0.5
        half_x = (-0.5 * wind_scale) * grad_y
        half_y = (0.5 * wind_scale) * grad_x
        half_z = (0.5 * vert_scale) * grad_z
        mixing = mix_base * (1.0 + 0.5 * jnp.tanh(theta))
        coef_ref[x, 0] = 1.0 - 6.0 * mixing
        coef_ref[x, 1] = mixing - half_x
        coef_ref[x, 2] = mixing + half_x
        coef_ref[x, 3] = jnp.where(last_y, mixing - half_y, 0.0)
        coef_ref[x, 4] = jnp.where(first_y, mixing + half_y, 0.0)
        coef_ref[x, 5] = jnp.where(last_z, mixing - half_z, 0.0)
        coef_ref[x, 6] = jnp.where(first_z, mixing + half_z, 0.0)
        return carry

    lax.fori_loop(0, length, body, 0, unroll=UNROLL)


def advance(coef_ref, state_ref, first_ref, length, count):
    nz, ny = state_ref.shape[-2:]

    def apply(source, x, east, west, i, coef):
        field = source[x, i]
        value = coef[0] * field + coef[1] * source[east, i] + coef[2] * source[west, i]
        value += coef[5] * pltpu.roll(field, nz - 1, 0) + coef[6] * pltpu.roll(field, 1, 0)
        value += coef[3] * pltpu.roll(field, ny - 1, 1) + coef[4] * pltpu.roll(field, 1, 1)
        return value

    def sweep(source, put):
        def body(x, carry):
            east = jnp.where(x == length - 1, 0, x + 1)
            west = jnp.where(x == 0, length - 1, x - 1)
            coef = [coef_ref[x, k] for k in range(7)]
            for i in range(count):
                put(x, i, apply(source, x, east, west, i, coef))
            return carry

        lax.fori_loop(0, length, body, 0, unroll=UNROLL)

    def put_first(x, i, value):
        first_ref[x, i] = value

    def put_state(x, i, value):
        state_ref[x, i] = state_ref[x, i] + value

    def step(_, carry):
        sweep(state_ref, put_first)
        sweep(first_ref, put_state)
        return carry

    lax.fori_loop(0, STEPS, step, 0)


def unpack(piece_ref, index, rows, nz, row):
    return piece_ref[index, pl.ds(row, nz, stride=rows), :]


def load(pieces, part, rows, nz, state_ref):
    for step, piece in enumerate(pieces):
        for row in range(rows):
            for i in range(part):
                state_ref[step * rows + row, i] = unpack(piece, i, rows, nz, row)


def store(outs, part, rows, nz, state_ref):
    for step, out in enumerate(outs):
        for row in range(rows):
            for i in range(part):
                out[i, pl.ds(row, nz, stride=rows), :] = state_ref[step * rows + row, i] * (SCALE * SCALE)


def dynamics(tiles, rows, nz, *refs):
    pieces, (coef_ref, next_ref, theta_out, theta_ref, state_ref, first_ref) = refs[:tiles], refs[tiles:]
    length = tiles * rows
    for step in range(tiles):
        for row in range(rows):
            theta_ref[step * rows + row] = unpack(pieces[step], 0, rows, nz, row)
            state_ref[step * rows + row, 0] = unpack(pieces[step], 1, rows, nz, row)
    coefficients(theta_ref, coef_ref, length)
    advance(coef_ref, state_ref, first_ref, length, 1)

    def heat(x, carry):
        theta_ref[x] = theta_ref[x] + (heat_step * SCALE) * state_ref[x, 0]
        return carry

    lax.fori_loop(0, length, heat, 0, unroll=UNROLL)
    coefficients(theta_ref, next_ref, length)
    advance(next_ref, state_ref, first_ref, length, 1)
    for row in range(rows):
        theta_out[pl.ds(row, nz, stride=rows), :] = theta_ref[row] + (heat_step * SCALE * SCALE) * state_ref[row, 0]


def both(tiles, part, rows, nz, *refs):
    pieces, (coef_ref, next_ref) = refs[:tiles], refs[tiles:tiles + 2]
    outs, (state_ref, first_ref) = refs[tiles + 2:2 * tiles + 2], refs[2 * tiles + 2:]
    load(pieces, part, rows, nz, state_ref)
    advance(coef_ref, state_ref, first_ref, tiles * rows, part)
    advance(next_ref, state_ref, first_ref, tiles * rows, part)
    store(outs, part, rows, nz, state_ref)


def assemble(tiles, parts, me_ref, *refs):
    pieces, out_ref, sem = refs[:-2], refs[-2], refs[-1]
    me = me_ref[0]
    share = sum(parts)
    copies = []
    for step in range(tiles):
        slot = lax.rem(me + tiles - step, tiles) * share
        for chunk, part in enumerate(parts):
            copies.append(pltpu.make_async_copy(pieces[chunk * tiles + step], out_ref.at[pl.ds(slot, part)], sem.at[len(copies)]))
            copies[-1].start()
            slot = slot + part
    for copy in copies:
        copy.wait()


def swap(value, axis, hop):
    return lax.ppermute(value, axis, [(i, i ^ hop) for i in range(lax.axis_size(axis))])


def per_device(theta, tracers, counts, flags, kappa):
    _, slots, nz, rows, ny = tracers.shape
    tiles = lax.axis_size("tile")
    share = max(2, -(-slots // tiles))
    parts = (share // 2, share - share // 2)
    length = tiles * rows
    me = lax.axis_index("tile").astype(jnp.int32).reshape(1)
    flat = (nz * rows, ny)
    f32 = jnp.float32
    field = lambda *lead: jax.ShapeDtypeStruct(lead, f32)
    scratch = lambda *lead: pltpu.VMEM(lead, f32)

    def shift(value, step):
        return lax.ppermute(value, "tile", [(i, (i + step) % tiles) for i in range(tiles)])

    def gather(payload):
        return [payload[0]] + [shift(payload[tiles - step], tiles - step) for step in range(1, tiles)]

    tracers = tracers[0].reshape(slots, *flat)
    theta = theta.reshape(flat)
    total = pl.pallas_call(
        functools.partial(weigh, slots),
        out_shape=field(*flat),
        in_specs=[SMEM, SMEM, SMEM, VMEM],
        out_specs=VMEM,
        compiler_params=params(),
        name="weigh",
    )(counts, flags, kappa, tracers)
    hop = 1
    while hop < lax.axis_size("group"):
        total = total + swap(total, "group", hop)
        hop *= 2
    small = jnp.stack([theta, total])
    small = [small] + [shift(small, tiles - step) for step in range(1, tiles)]

    def pack(before, part, after):
        return pl.pallas_call(
            functools.partial(pack_two, tiles, share, before, part, slots),
            out_shape=[field(part, *flat)] * tiles,
            in_specs=[SMEM, SMEM, VMEM, HBM],
            out_specs=[VMEM] * tiles,
            compiler_params=params(),
            name="pack",
        )(me, counts, tracers, after)

    payload = pack(0, parts[0], me)
    one = gather(payload)
    two = gather(pack(parts[0], parts[1], payload[0]))
    coef, next_coef, theta_new = pl.pallas_call(
        functools.partial(dynamics, tiles, rows, nz),
        out_shape=[field(length, 7, nz, ny), field(length, 7, nz, ny), field(*flat)],
        in_specs=[VMEM] * tiles,
        out_specs=[VMEM] * 3,
        scratch_shapes=[scratch(length, nz, ny), scratch(length, 1, nz, ny), scratch(length, 1, nz, ny)],
        compiler_params=params(),
        name="dynamics",
    )(*small)

    def work(pieces, part):
        return pl.pallas_call(
            functools.partial(both, tiles, part, rows, nz),
            out_shape=[field(part, *flat)] * tiles,
            in_specs=[VMEM] * (tiles + 2),
            out_specs=[VMEM] * tiles,
            scratch_shapes=[scratch(length, part, nz, ny)] * 2,
            compiler_params=params(),
            name="both",
        )(*pieces, coef, next_coef)

    done_one = work(one, parts[0])
    done_two = work(two, parts[1])
    back = [piece for done in (done_one, done_two) for piece in [done[0]] + [shift(done[step], step) for step in range(1, tiles)]]
    out = pl.pallas_call(
        functools.partial(assemble, tiles, parts),
        out_shape=field(tiles * share, *flat),
        in_specs=[SMEM] + [VMEM] * (2 * tiles),
        out_specs=HBM,
        scratch_shapes=[pltpu.SemaphoreType.DMA((2 * tiles,))],
        compiler_params=params(),
        name="assemble",
    )(me, *back)
    return theta_new.reshape(nz, rows, ny), out[:slots].reshape(1, slots, nz, rows, ny)


def solution(mesh):
    return jax.shard_map(
        per_device,
        mesh=mesh,
        in_specs=(
            P("members", "tile", None),
            P("group", "members", None, "tile", None),
            P("group", "members"),
            P("group", "members"),
            P("group", None),
        ),
        out_specs=(P("members", "tile", None), P("group", "members", None, "tile", None)),
        check_vma=False,
    )
```

```python
import functools
import jax
import jax.numpy as jnp
from jax import lax
from jax.experimental import pallas as pl
from jax.experimental.pallas import tpu as pltpu
from jax.sharding import PartitionSpec as P

STEPS = 3
INTERVALS = 2

wind_scale = 0.3
vert_scale = 0.2
mix_base = 0.08
heat_step = 0.3

UNROLL = 16
SCALE = 0.5 ** STEPS

VMEM = pl.BlockSpec(memory_space=pltpu.VMEM)
SMEM = pl.BlockSpec(memory_space=pltpu.SMEM)
HBM = pl.BlockSpec(memory_space=pl.ANY)


def params():
    return pltpu.CompilerParams(vmem_limit_bytes=48 * 1024 * 1024)


def weigh(slots, counts_ref, flags_ref, kappa_ref, tracers_ref, total_ref):
    count = counts_ref[0, 0]
    totals = [jnp.zeros(total_ref.shape, jnp.float32)] * 4
    for slot in range(slots):
        weight = jnp.where(slot < count, flags_ref[0, slot].astype(jnp.float32) * kappa_ref[0, slot], 0.0)
        totals[slot % 4] = totals[slot % 4] + weight * tracers_ref[slot]
    total_ref[...] = (totals[0] + totals[1]) + (totals[2] + totals[3])


def sort_slots(tiles, share, first, part, slots, me_ref, counts_ref, tracers_ref, outs):
    me = me_ref[0]
    count = counts_ref[0, 0]
    for step in range(tiles):
        block = lax.rem(me + step, tiles) * share + first
        for i in range(part):
            slot = block + i
            safe = jnp.minimum(slot, slots - 1)
            outs[step][i] = tracers_ref[safe] * jnp.where(slot < count, 1.0, 0.0)


def pack_two(tiles, share, first, part, slots, me_ref, counts_ref, tracers_ref, after_ref, *outs):
    sort_slots(tiles, share, first, part, slots, me_ref, counts_ref, tracers_ref, outs)


def coefficients(theta_ref, coef_ref, length):
    shape = theta_ref.shape[1:]
    level = lax.broadcasted_iota(jnp.int32, shape, 0)
    place = lax.broadcasted_iota(jnp.int32, shape, 1)
    nz, ny = shape
    first_y, last_y = place > 0, place < ny - 1
    first_z, last_z = level > 0, level < nz - 1

    def body(x, carry):
        east = jnp.where(x == length - 1, 0, x + 1)
        west = jnp.where(x == 0, length - 1, x - 1)
        theta = theta_ref[x]
        grad_x = (theta_ref[east] - theta_ref[west]) * 0.5
        grad_y = (jnp.where(last_y, pltpu.roll(theta, ny - 1, 1), 0.0) - jnp.where(first_y, pltpu.roll(theta, 1, 1), 0.0)) * 0.5
        grad_z = (jnp.where(last_z, pltpu.roll(theta, nz - 1, 0), 0.0) - jnp.where(first_z, pltpu.roll(theta, 1, 0), 0.0)) * 0.5
        half_x = (-0.5 * wind_scale) * grad_y
        half_y = (0.5 * wind_scale) * grad_x
        half_z = (0.5 * vert_scale) * grad_z
        mixing = mix_base * (1.0 + 0.5 * jnp.tanh(theta))
        coef_ref[x, 0] = 1.0 - 6.0 * mixing
        coef_ref[x, 1] = mixing - half_x
        coef_ref[x, 2] = mixing + half_x
        coef_ref[x, 3] = jnp.where(last_y, mixing - half_y, 0.0)
        coef_ref[x, 4] = jnp.where(first_y, mixing + half_y, 0.0)
        coef_ref[x, 5] = jnp.where(last_z, mixing - half_z, 0.0)
        coef_ref[x, 6] = jnp.where(first_z, mixing + half_z, 0.0)
        return carry

    lax.fori_loop(0, length, body, 0, unroll=UNROLL)


def advance(coef_ref, state_ref, first_ref, length, count):
    nz, ny = state_ref.shape[-2:]

    def apply(source, x, east, west, i, coef):
        field = source[x, i]
        value = coef[0] * field + coef[1] * source[east, i] + coef[2] * source[west, i]
        value += coef[5] * pltpu.roll(field, nz - 1, 0) + coef[6] * pltpu.roll(field, 1, 0)
        value += coef[3] * pltpu.roll(field, ny - 1, 1) + coef[4] * pltpu.roll(field, 1, 1)
        return value

    def sweep(source, put):
        def body(x, carry):
            east = jnp.where(x == length - 1, 0, x + 1)
            west = jnp.where(x == 0, length - 1, x - 1)
            coef = [coef_ref[x, k] for k in range(7)]
            for i in range(count):
                put(x, i, apply(source, x, east, west, i, coef))
            return carry

        lax.fori_loop(0, length, body, 0, unroll=UNROLL)

    def put_first(x, i, value):
        first_ref[x, i] = value

    def put_state(x, i, value):
        state_ref[x, i] = state_ref[x, i] + value

    def step(_, carry):
        sweep(state_ref, put_first)
        sweep(first_ref, put_state)
        return carry

    lax.fori_loop(0, STEPS, step, 0)


def unpack(piece_ref, index, rows, nz, row):
    return piece_ref[index, pl.ds(row, nz, stride=rows), :]


def load(pieces, part, rows, nz, state_ref):
    for step, piece in enumerate(pieces):
        for row in range(rows):
            for i in range(part):
                state_ref[step * rows + row, i] = unpack(piece, i, rows, nz, row)


def store(outs, part, rows, nz, state_ref):
    for step, out in enumerate(outs):
        for row in range(rows):
            for i in range(part):
                out[i, pl.ds(row, nz, stride=rows), :] = state_ref[step * rows + row, i] * (SCALE * SCALE)


def dynamics(tiles, rows, nz, *refs):
    pieces, (coef_ref, next_ref, theta_out, theta_ref, state_ref, first_ref) = refs[:tiles], refs[tiles:]
    length = tiles * rows
    for step in range(tiles):
        for row in range(rows):
            theta_ref[step * rows + row] = unpack(pieces[step], 0, rows, nz, row)
            state_ref[step * rows + row, 0] = unpack(pieces[step], 1, rows, nz, row)
    coefficients(theta_ref, coef_ref, length)
    advance(coef_ref, state_ref, first_ref, length, 1)

    def heat(x, carry):
        theta_ref[x] = theta_ref[x] + (heat_step * SCALE) * state_ref[x, 0]
        return carry

    lax.fori_loop(0, length, heat, 0, unroll=UNROLL)
    coefficients(theta_ref, next_ref, length)
    advance(next_ref, state_ref, first_ref, length, 1)
    for row in range(rows):
        theta_out[pl.ds(row, nz, stride=rows), :] = theta_ref[row] + (heat_step * SCALE * SCALE) * state_ref[row, 0]


def both(tiles, part, rows, nz, *refs):
    pieces, (coef_ref, next_ref) = refs[:tiles], refs[tiles:tiles + 2]
    outs, (state_ref, first_ref) = refs[tiles + 2:2 * tiles + 2], refs[2 * tiles + 2:]
    load(pieces, part, rows, nz, state_ref)
    advance(coef_ref, state_ref, first_ref, tiles * rows, part)
    advance(next_ref, state_ref, first_ref, tiles * rows, part)
    store(outs, part, rows, nz, state_ref)


def assemble(tiles, parts, me_ref, *refs):
    pieces, out_ref, sem = refs[:-2], refs[-2], refs[-1]
    me = me_ref[0]
    share = sum(parts)
    copies = []
    for step in range(tiles):
        slot = lax.rem(me + tiles - step, tiles) * share
        for chunk, part in enumerate(parts):
            copies.append(pltpu.make_async_copy(pieces[chunk * tiles + step], out_ref.at[pl.ds(slot, part)], sem.at[len(copies)]))
            copies[-1].start()
            slot = slot + part
    for copy in copies:
        copy.wait()


def swap(value, axis, hop):
    return lax.ppermute(value, axis, [(i, i ^ hop) for i in range(lax.axis_size(axis))])


def per_device(theta, tracers, counts, flags, kappa):
    _, slots, nz, rows, ny = tracers.shape
    tiles = lax.axis_size("tile")
    share = max(2, -(-slots // tiles))
    parts = (share // 2, share - share // 2)
    length = tiles * rows
    me = lax.axis_index("tile").astype(jnp.int32).reshape(1)
    flat = (nz * rows, ny)
    f32 = jnp.float32
    field = lambda *lead: jax.ShapeDtypeStruct(lead, f32)
    scratch = lambda *lead: pltpu.VMEM(lead, f32)

    def shift(value, step):
        return lax.ppermute(value, "tile", [(i, (i + step) % tiles) for i in range(tiles)])

    def gather(payload):
        return [payload[0]] + [shift(payload[tiles - step], tiles - step) for step in range(1, tiles)]

    tracers = tracers[0].reshape(slots, *flat)
    theta = theta.reshape(flat)
    total = pl.pallas_call(
        functools.partial(weigh, slots),
        out_shape=field(*flat),
        in_specs=[SMEM, SMEM, SMEM, VMEM],
        out_specs=VMEM,
        compiler_params=pltpu.CompilerParams(vmem_limit_bytes=63 * 1024 * 1024),
        name="weigh",
    )(counts, flags, kappa, tracers)
    total = sum((swap(total, "group", hop) for hop in range(1, lax.axis_size("group"))), total)
    small = jnp.stack([theta, total])
    small = [small] + [shift(small, tiles - step) for step in range(1, tiles)]

    def pack(before, part, after):
        return pl.pallas_call(
            functools.partial(pack_two, tiles, share, before, part, slots),
            out_shape=[field(part, *flat)] * tiles,
            in_specs=[SMEM, SMEM, VMEM, HBM],
            out_specs=[VMEM] * tiles,
            compiler_params=params(),
            name="pack",
        )(me, counts, tracers, after)

    payload = pack(0, parts[0], me)
    one = gather(payload)
    two = gather(pack(parts[0], parts[1], payload[0]))
    coef, next_coef, theta_new = pl.pallas_call(
        functools.partial(dynamics, tiles, rows, nz),
        out_shape=[field(length, 7, nz, ny), field(length, 7, nz, ny), field(*flat)],
        in_specs=[VMEM] * tiles,
        out_specs=[VMEM] * 3,
        scratch_shapes=[scratch(length, nz, ny), scratch(length, 1, nz, ny), scratch(length, 1, nz, ny)],
        compiler_params=params(),
        name="dynamics",
    )(*small)

    def work(pieces, part):
        return pl.pallas_call(
            functools.partial(both, tiles, part, rows, nz),
            out_shape=[field(part, *flat)] * tiles,
            in_specs=[VMEM] * (tiles + 2),
            out_specs=[VMEM] * tiles,
            scratch_shapes=[scratch(length, part, nz, ny)] * 2,
            compiler_params=params(),
            name="both",
        )(*pieces, coef, next_coef)

    done_one = work(one, parts[0])
    done_two = work(two, parts[1])
    back = [piece for done in (done_one, done_two) for piece in [done[0]] + [shift(done[step], step) for step in range(1, tiles)]]
    out = pl.pallas_call(
        functools.partial(assemble, tiles, parts),
        out_shape=field(tiles * share, *flat),
        in_specs=[SMEM] + [VMEM] * (2 * tiles),
        out_specs=HBM,
        scratch_shapes=[pltpu.SemaphoreType.DMA((2 * tiles,))],
        compiler_params=params(),
        name="assemble",
    )(me, *back)
    return theta_new.reshape(nz, rows, ny), out[:slots].reshape(1, slots, nz, rows, ny)


def solution(mesh):
    return jax.shard_map(
        per_device,
        mesh=mesh,
        in_specs=(
            P("members", "tile", None),
            P("group", "members", None, "tile", None),
            P("group", "members"),
            P("group", "members"),
            P("group", None),
        ),
        out_specs=(P("members", "tile", None), P("group", "members", None, "tile", None)),
        check_vma=False,
    )
```

```python
import functools
import jax
import jax.numpy as jnp
from jax import lax
from jax.experimental import pallas as pl
from jax.experimental.pallas import tpu as pltpu
from jax.sharding import PartitionSpec as P

STEPS = 3
INTERVALS = 2

wind_scale = 0.3
vert_scale = 0.2
mix_base = 0.08
heat_step = 0.3

UNROLL = 16
SCALE = 0.5 ** STEPS

VMEM = pl.BlockSpec(memory_space=pltpu.VMEM)
SMEM = pl.BlockSpec(memory_space=pltpu.SMEM)
HBM = pl.BlockSpec(memory_space=pl.ANY)


def params():
    return pltpu.CompilerParams(vmem_limit_bytes=48 * 1024 * 1024)


def weigh(slots, counts_ref, flags_ref, kappa_ref, tracers_ref, total_ref):
    count = counts_ref[0, 0]
    totals = [jnp.zeros(total_ref.shape, jnp.float32)] * 4
    for slot in range(slots):
        weight = jnp.where(slot < count, flags_ref[0, slot].astype(jnp.float32) * kappa_ref[0, slot], 0.0)
        totals[slot % 4] = totals[slot % 4] + weight * tracers_ref[slot]
    total_ref[...] = (totals[0] + totals[1]) + (totals[2] + totals[3])


def sort_slots(tiles, share, first, part, slots, me_ref, counts_ref, tracers_ref, outs):
    me = me_ref[0]
    count = counts_ref[0, 0]
    for step in range(tiles):
        block = lax.rem(me + step, tiles) * share + first
        for i in range(part):
            slot = block + i
            safe = jnp.minimum(slot, slots - 1)
            outs[step][i] = tracers_ref[safe] * jnp.where(slot < count, 1.0, 0.0)


def pack_two(tiles, share, first, part, slots, me_ref, counts_ref, tracers_ref, after_ref, *outs):
    sort_slots(tiles, share, first, part, slots, me_ref, counts_ref, tracers_ref, outs)


def coefficients(theta_ref, coef_ref, length):
    shape = theta_ref.shape[1:]
    level = lax.broadcasted_iota(jnp.int32, shape, 0)
    place = lax.broadcasted_iota(jnp.int32, shape, 1)
    nz, ny = shape
    first_y, last_y = place > 0, place < ny - 1
    first_z, last_z = level > 0, level < nz - 1

    def body(x, carry):
        east = jnp.where(x == length - 1, 0, x + 1)
        west = jnp.where(x == 0, length - 1, x - 1)
        theta = theta_ref[x]
        grad_x = (theta_ref[east] - theta_ref[west]) * 0.5
        grad_y = (jnp.where(last_y, pltpu.roll(theta, ny - 1, 1), 0.0) - jnp.where(first_y, pltpu.roll(theta, 1, 1), 0.0)) * 0.5
        grad_z = (jnp.where(last_z, pltpu.roll(theta, nz - 1, 0), 0.0) - jnp.where(first_z, pltpu.roll(theta, 1, 0), 0.0)) * 0.5
        half_x = (-0.5 * wind_scale) * grad_y
        half_y = (0.5 * wind_scale) * grad_x
        half_z = (0.5 * vert_scale) * grad_z
        mixing = mix_base * (1.0 + 0.5 * jnp.tanh(theta))
        coef_ref[x, 0] = 1.0 - 6.0 * mixing
        coef_ref[x, 1] = mixing - half_x
        coef_ref[x, 2] = mixing + half_x
        coef_ref[x, 3] = jnp.where(last_y, mixing - half_y, 0.0)
        coef_ref[x, 4] = jnp.where(first_y, mixing + half_y, 0.0)
        coef_ref[x, 5] = jnp.where(last_z, mixing - half_z, 0.0)
        coef_ref[x, 6] = jnp.where(first_z, mixing + half_z, 0.0)
        return carry

    lax.fori_loop(0, length, body, 0, unroll=UNROLL)


def advance(coef_ref, state_ref, first_ref, length, count):
    nz, ny = state_ref.shape[-2:]

    def apply(source, x, east, west, i, coef):
        field = source[x, i]
        value = coef[0] * field + coef[1] * source[east, i] + coef[2] * source[west, i]
        value += coef[5] * pltpu.roll(field, nz - 1, 0) + coef[6] * pltpu.roll(field, 1, 0)
        value += coef[3] * pltpu.roll(field, ny - 1, 1) + coef[4] * pltpu.roll(field, 1, 1)
        return value

    def sweep(source, put):
        def body(x, carry):
            east = jnp.where(x == length - 1, 0, x + 1)
            west = jnp.where(x == 0, length - 1, x - 1)
            coef = [coef_ref[x, k] for k in range(7)]
            for i in range(count):
                put(x, i, apply(source, x, east, west, i, coef))
            return carry

        lax.fori_loop(0, length, body, 0, unroll=UNROLL)

    def put_first(x, i, value):
        first_ref[x, i] = value

    def put_state(x, i, value):
        state_ref[x, i] = state_ref[x, i] + value

    def step(_, carry):
        sweep(state_ref, put_first)
        sweep(first_ref, put_state)
        return carry

    lax.fori_loop(0, STEPS, step, 0)


def unpack(piece_ref, index, rows, nz, row):
    return piece_ref[index, pl.ds(row, nz, stride=rows), :]


def load(pieces, part, rows, nz, state_ref):
    for step, piece in enumerate(pieces):
        for row in range(rows):
            for i in range(part):
                state_ref[step * rows + row, i] = unpack(piece, i, rows, nz, row)


def store(outs, part, rows, nz, state_ref):
    for step, out in enumerate(outs):
        for row in range(rows):
            for i in range(part):
                out[i, pl.ds(row, nz, stride=rows), :] = state_ref[step * rows + row, i] * (SCALE * SCALE)


def dynamics(tiles, rows, nz, *refs):
    pieces, (coef_ref, next_ref, theta_ref, state_ref, first_ref) = refs[:tiles], refs[tiles:]
    length = tiles * rows
    for step in range(tiles):
        for row in range(rows):
            theta_ref[step * rows + row] = unpack(pieces[step], 0, rows, nz, row)
            state_ref[step * rows + row, 0] = unpack(pieces[step], 1, rows, nz, row)
    coefficients(theta_ref, coef_ref, length)
    advance(coef_ref, state_ref, first_ref, length, 1)

    def heat(x, carry):
        theta_ref[x] = theta_ref[x] + (heat_step * SCALE) * state_ref[x, 0]
        return carry

    lax.fori_loop(0, length, heat, 0, unroll=UNROLL)
    coefficients(theta_ref, next_ref, length)


def finish(rows, nz, theta_ref, total_ref, next_ref, after_ref, theta_out, state_ref, first_ref):
    length = total_ref.shape[0]

    def copy(x, carry):
        state_ref[x, 0] = total_ref[x, 0]
        return carry

    lax.fori_loop(0, length, copy, 0, unroll=UNROLL)
    advance(next_ref, state_ref, first_ref, length, 1)
    for row in range(rows):
        theta_out[pl.ds(row, nz, stride=rows), :] = theta_ref[row] + (heat_step * SCALE * SCALE) * state_ref[row, 0]


def both(tiles, part, rows, nz, *refs):
    pieces, (coef_ref, next_ref) = refs[:tiles], refs[tiles:tiles + 2]
    outs, (state_ref, first_ref) = refs[tiles + 2:2 * tiles + 2], refs[2 * tiles + 2:]
    load(pieces, part, rows, nz, state_ref)
    advance(coef_ref, state_ref, first_ref, tiles * rows, part)
    advance(next_ref, state_ref, first_ref, tiles * rows, part)
    store(outs, part, rows, nz, state_ref)


def assemble(tiles, parts, me_ref, *refs):
    pieces, out_ref, sem = refs[:-2], refs[-2], refs[-1]
    me = me_ref[0]
    share = sum(parts)
    copies = []
    for step in range(tiles):
        slot = lax.rem(me + tiles - step, tiles) * share
        for chunk, part in enumerate(parts):
            copies.append(pltpu.make_async_copy(pieces[chunk * tiles + step], out_ref.at[pl.ds(slot, part)], sem.at[len(copies)]))
            copies[-1].start()
            slot = slot + part
    for copy in copies:
        copy.wait()


def swap(value, axis, hop):
    return lax.ppermute(value, axis, [(i, i ^ hop) for i in range(lax.axis_size(axis))])


def per_device(theta, tracers, counts, flags, kappa):
    _, slots, nz, rows, ny = tracers.shape
    tiles = lax.axis_size("tile")
    share = max(2, -(-slots // tiles))
    first = max(1, share * 6 // 12)
    parts = (first, share - first)
    length = tiles * rows
    me = lax.axis_index("tile").astype(jnp.int32).reshape(1)
    flat = (nz * rows, ny)
    f32 = jnp.float32
    field = lambda *lead: jax.ShapeDtypeStruct(lead, f32)
    scratch = lambda *lead: pltpu.VMEM(lead, f32)

    def shift(value, step):
        return lax.ppermute(value, "tile", [(i, (i + step) % tiles) for i in range(tiles)])

    def gather(payload):
        return [payload[0]] + [shift(payload[tiles - step], tiles - step) for step in range(1, tiles)]

    tracers = tracers[0].reshape(slots, *flat)
    theta = theta.reshape(flat)
    total = pl.pallas_call(
        functools.partial(weigh, slots),
        out_shape=field(*flat),
        in_specs=[SMEM, SMEM, SMEM, VMEM],
        out_specs=VMEM,
        compiler_params=pltpu.CompilerParams(vmem_limit_bytes=63 * 1024 * 1024),
        name="weigh",
    )(counts, flags, kappa, tracers)
    total = sum((swap(total, "group", hop) for hop in range(1, lax.axis_size("group"))), total)
    small = jnp.stack([theta, total])
    small = [small] + [shift(small, tiles - step) for step in range(1, tiles)]

    def pack(before, part, after):
        return pl.pallas_call(
            functools.partial(pack_two, tiles, share, before, part, slots),
            out_shape=[field(part, *flat)] * tiles,
            in_specs=[SMEM, SMEM, VMEM, HBM],
            out_specs=[VMEM] * tiles,
            compiler_params=params(),
            name="pack",
        )(me, counts, tracers, after)

    payload = pack(0, parts[0], me)
    one = gather(payload)
    two = gather(pack(parts[0], parts[1], me))
    coef, next_coef, theta_mid, total_mid = pl.pallas_call(
        functools.partial(dynamics, tiles, rows, nz),
        out_shape=[field(length, 7, nz, ny), field(length, 7, nz, ny), field(length, nz, ny), field(length, 1, nz, ny)],
        in_specs=[VMEM] * tiles,
        out_specs=[VMEM] * 4,
        scratch_shapes=[scratch(length, 1, nz, ny)],
        compiler_params=params(),
        name="dynamics",
    )(*small)

    def work(pieces, part):
        return pl.pallas_call(
            functools.partial(both, tiles, part, rows, nz),
            out_shape=[field(part, *flat)] * tiles,
            in_specs=[VMEM] * (tiles + 2),
            out_specs=[VMEM] * tiles,
            scratch_shapes=[scratch(length, part, nz, ny)] * 2,
            compiler_params=params(),
            name="both",
        )(*pieces, coef, next_coef)

    done_one = work(one, parts[0])
    done_two = work(two, parts[1])
    theta_new = pl.pallas_call(
        functools.partial(finish, rows, nz),
        out_shape=field(*flat),
        in_specs=[VMEM] * 3 + [HBM],
        out_specs=VMEM,
        scratch_shapes=[scratch(length, 1, nz, ny)] * 2,
        compiler_params=params(),
        name="finish",
    )(theta_mid, total_mid, next_coef, done_one[0])
    back = [piece for done in (done_one, done_two) for piece in [done[0]] + [shift(done[step], step) for step in range(1, tiles)]]
    out = pl.pallas_call(
        functools.partial(assemble, tiles, parts),
        out_shape=field(tiles * share, *flat),
        in_specs=[SMEM] + [VMEM] * (2 * tiles),
        out_specs=HBM,
        scratch_shapes=[pltpu.SemaphoreType.DMA((2 * tiles,))],
        compiler_params=params(),
        name="assemble",
    )(me, *back)
    return theta_new.reshape(nz, rows, ny), out[:slots].reshape(1, slots, nz, rows, ny)


def solution(mesh):
    return jax.shard_map(
        per_device,
        mesh=mesh,
        in_specs=(
            P("members", "tile", None),
            P("group", "members", None, "tile", None),
            P("group", "members"),
            P("group", "members"),
            P("group", None),
        ),
        out_specs=(P("members", "tile", None), P("group", "members", None, "tile", None)),
        check_vma=False,
    )
```
